32 devices in a mesh: lat: 4 (over y, x), lon: 8 (over z, core).
Axes of the slice: x: 2, y: 2, z: 4, core: 2. Of those that a mesh axis runs over, the one named last changes fastest.
Arguments:
- tracers: float32 [2, 3, 1024, 1024], P(None, None, 'lat', 'lon'), may hold values from -6 to 6
- east_courant: float32 [3, 1024, 1024], P(None, 'lat', 'lon'), may hold values from -0.45 to 0.45
- north_courant: float32 [3, 1024, 1024], P(None, 'lat', 'lon'), may hold values from -0.45 to 0.45
- east_kappa: float32 [3, 1024, 1024], P(None, 'lat', 'lon'), may hold values from 0.01 to 0.1
- north_kappa: float32 [3, 1024, 1024], P(None, 'lat', 'lon'), may hold values from 0.01 to 0.1
- ocean_mask: int32 [3, 1024, 1024], P(None, 'lat', 'lon'), may hold values 0 or 1
- fold_map: int32 [1024], P('lon'), may hold values from 0 to 1023, as said below
Outputs:
- updated: float32 [2, 3, 1024, 1024], P(None, None, 'lat', 'lon')
The draws below stay inside these ranges and needn't reach their ends.
Inputs may be any that keep to these rules, and one draw needn't show every extreme that they name: fold_map[i] = (P - 1 - i) mod 1024 for every column i, with one pivot P that is a multiple of 128.
All inputs are finite; a program needn't handle non-finite values. No bound on the sum of `ocean_mask` on one device may be relied on, other than what follows from the above.
Results may differ from the reference program's by a relative error of at most 0.00002.
Values sent between devices are 32-bit elements; how exact they have to be, the bound alone decides.
A program may use at most 64 MiB of HBM per device.

```python
import math
import jax
import jax.numpy as jnp
from jax import lax

LEV = 3
STEPS = 2
CLON = 128
NY = 1024
NX = 1024


def draw_fold_map(key, part):
    blocks = NX // CLON
    pivot = jax.random.randint(key, (), 0, blocks, dtype=jnp.int32) * CLON
    column = jnp.arange(NX, dtype=jnp.int32)
    return ((pivot - 1 - column) % NX).astype(jnp.int32)


def plant(values, rng, low, largest):
    dims = values.shape
    place = [jax.random.randint(jax.random.fold_in(rng, axis), (), 0, dims[axis]) for axis in range(len(dims))]
    values = values.at[tuple(place)].set(low)
    longest = dims.index(max(dims))
    place[longest] = (place[longest] + 1) % dims[longest]
    return values.at[tuple(place)].set(largest)


def steps_of(rng, extent, shards, smallest, largest):
    def one(position, parts):
        heights = jax.random.uniform(jax.random.fold_in(jax.random.fold_in(rng, 6), position), (parts,), jnp.float32, smallest / len(shards), largest / len(shards))
        return jnp.repeat(jnp.exp(heights), extent[position] // parts).reshape((-1,) + (1,) * (len(extent) - position - 1))

    gain = one(*shards[0])
    for cut in shards[1:]:
        gain = gain * one(*cut)
    return gain


def normal_values(stream_key, dims, deviation, reach, cuts=(), kind=jnp.bfloat16):
    level = steps_of(stream_key, dims, cuts, -0.22, 0.18) if cuts else 1.0
    drawn = jax.random.normal(stream_key, dims, jnp.float32) * deviation * level
    return jnp.minimum(jnp.maximum(drawn, -reach), reach).astype(kind)


def setup_inputs(seed: int = 0) -> dict:
    keys = jax.random.split(jax.random.key(seed), 8)
    tracers = normal_values(keys[0], (2, LEV, NY, NX), 1.0, 6.0, ((2, 4), (3, 8)), jnp.float32)
    east_courant = jnp.clip(jax.random.uniform(keys[1], (LEV, NY, NX), jnp.float32, -0.45, 0.45) * steps_of(keys[1], (LEV, NY, NX), ((1, 4), (2, 8)), -0.4, 0.0), -0.45, 0.45)
    north_courant = jnp.clip(jax.random.uniform(keys[2], (LEV, NY, NX), jnp.float32, -0.45, 0.45) * steps_of(keys[2], (LEV, NY, NX), ((1, 4), (2, 8)), -0.4, 0.0), -0.45, 0.45)
    east_kappa = jnp.clip(jnp.exp(math.log(0.1) - 2.3025851 * jax.random.uniform(keys[3], (LEV, NY, NX), jnp.float32) ** steps_of(keys[3], (LEV, NY, NX), ((1, 4), (2, 8)), -0.2, 0.2)), 0.01, 0.1)
    north_kappa = jnp.clip(jnp.exp(math.log(0.1) - 2.3025851 * jax.random.uniform(keys[4], (LEV, NY, NX), jnp.float32) ** steps_of(keys[4], (LEV, NY, NX), ((1, 4), (2, 8)), -0.2, 0.2)), 0.01, 0.1)
    ocean_mask = plant((jax.random.randint(keys[5], (LEV, NY, NX), 0, 5) < 4).astype(jnp.int32), jax.random.fold_in(keys[5], 1), 0, 1)
    fold_map = draw_fold_map(jax.random.fold_in(keys[7], 71), 0)
    return {"tracers": tracers, "east_courant": east_courant, "north_courant": north_courant, "east_kappa": east_kappa, "north_kappa": north_kappa, "ocean_mask": ocean_mask, "fold_map": fold_map}


def face_flux(behind, center, forward, beyond, courant, diffusivity, opened):
    centered = 7.0 * (center + forward) - (behind + beyond)
    upwind = 3.0 * (forward - center) - (beyond - behind)
    return opened * (courant * centered / 12.0 - jnp.abs(courant) * upwind / 12.0 - diffusivity * (forward - center))


def advance(state, ocean, east_c, east_k, open_east, north_c, north_k, open_north, fold_map):
    width = state.shape[2]
    along = jnp.concatenate([state[:, :, -2:], state, state[:, :, :2]], axis=2)
    folded = jnp.stack([state[:, -1, :][:, fold_map], state[:, -2, :][:, fold_map]], axis=1)
    across = jnp.concatenate([jnp.zeros((2, 2, width), jnp.float32), state, folded], axis=1)
    east_flux = face_flux(along[:, :, :-3], along[:, :, 1:-2], along[:, :, 2:-1], along[:, :, 3:], east_c, east_k, open_east)
    north_flux = face_flux(across[:, :-3], across[:, 1:-2], across[:, 2:-1], across[:, 3:], north_c, north_k, open_north)
    return ocean * (state - (east_flux[:, :, 1:] - east_flux[:, :, :-1]) - (north_flux[:, 1:] - north_flux[:, :-1]))


def reference(tracers, east_courant, north_courant, east_kappa, north_kappa, ocean_mask, fold_map):
    def one_level(level_index):
        def pick(field):
            return lax.dynamic_index_in_dim(field, level_index, 0, keepdims=False)

        state = lax.dynamic_index_in_dim(tracers, level_index, 1, keepdims=False)
        ocean = pick(ocean_mask).astype(jnp.float32)
        width = ocean.shape[1]
        zero_row = jnp.zeros((1, width), jnp.float32)
        east_cour = pick(east_courant)
        east_diff = pick(east_kappa)
        east_c = jnp.concatenate([east_cour[:, -1:], east_cour], axis=1)
        east_k = jnp.concatenate([east_diff[:, -1:], east_diff], axis=1)
        beside = jnp.concatenate([ocean[:, -1:], ocean, ocean[:, :1]], axis=1)
        open_east = beside[:, :-1] * beside[:, 1:]
        north_c = jnp.concatenate([zero_row, pick(north_courant)], axis=0)
        north_k = jnp.concatenate([zero_row, pick(north_kappa)], axis=0)
        vertical = jnp.concatenate([zero_row, ocean, ocean[-1:]], axis=0)
        open_north = vertical[:-1] * vertical[1:]
        state = state * ocean
        for step_index in range(STEPS):
            state = advance(state, ocean, east_c, east_k, open_east, north_c, north_k, open_north, fold_map)
        return state

    result = lax.map(one_level, jnp.arange(LEV, dtype=jnp.int32))
    return jnp.transpose(result, (1, 0, 2, 3))
```

```python
import functools

import jax
import jax.numpy as jnp
from jax import lax
from jax.experimental import pallas as pl
from jax.experimental.pallas import tpu as pltpu
from jax.sharding import PartitionSpec as P

MESH = pl.DeviceIdType.MESH
F32 = jnp.float32
TOP = 16
BLOCK = 64


def face_flux(behind, center, forward, beyond, courant, diffusivity, opened):
    centered = 7.0 * (center + forward) - (behind + beyond)
    upwind = 3.0 * (forward - center) - (beyond - behind)
    return opened * (
        courant * centered * (1.0 / 12.0)
        - jnp.abs(courant) * upwind * (1.0 / 12.0)
        - diffusivity * (forward - center)
    )


def face_weights(courant, diffusivity, opened):
    ahead = courant >= 0.0
    scaled = opened * courant * (1.0 / 6.0)
    spread = opened * diffusivity
    center = scaled * jnp.where(ahead, 5.0, 2.0) + spread
    forward = scaled * jnp.where(ahead, 2.0, 5.0) - spread
    return ahead, center, forward, -scaled


def reversed_lanes(values):
    lane = lax.broadcasted_iota(jnp.int32, values.shape, values.ndim - 1)
    axis = values.ndim - 1
    step = values.shape[-1] // 2
    while step:
        up = pltpu.roll(values, values.shape[-1] - step, axis)
        down = pltpu.roll(values, step, axis)
        values = jnp.where((lane & step) == 0, up, down)
        step //= 2
    return values


def kernel(
    nlat, nlon, fold_ref, tr, ec, nc, ek, nk, mask, out,
    s0, s1, ocean, we, wn, packed, t0, t1, ct, ce,
    se, sw, sn, ss, sf, re, rw, rn, rs, rf0, rf1, north_rows,
    send_sem, recv_sem, fold_send, fold_recv,
):
    levels, rows, cols = mask.shape
    lat = lax.axis_index("lat")
    lon = lax.axis_index("lon")
    southern = lat == 0
    northern = lat == nlat - 1
    east = lax.rem(lon + 1, nlon)
    west = lax.rem(lon + nlon - 1, nlon)
    barrier = pltpu.get_barrier_semaphore()
    rf = (rf0, rf1)

    def greet(a, b):
        pl.semaphore_signal(barrier, inc=1, device_id=(a, b), device_id_type=MESH)

    greet(lat, east)
    greet(lat, west)

    @pl.when(jnp.logical_not(southern))
    def _():
        greet(lat - 1, lon)

    @pl.when(jnp.logical_not(northern))
    def _():
        greet(lat + 1, lon)

    @pl.when(northern)
    def _():
        for d in range(2, nlon - 1):
            greet(lat, lax.rem(lon + d, nlon))

    lane = lax.broadcasted_iota(jnp.int32, (BLOCK, cols), 1)
    starts = range(0, rows, BLOCK)

    def level_setup(l, carry):
        for r in starts:
            o = mask[l, r : r + BLOCK, :].astype(F32)
            ocean[l, r : r + BLOCK, :] = o
            for t in range(2):
                s0[t * levels + l, TOP + r : TOP + r + BLOCK, :] = tr[t, l, r : r + BLOCK, :] * o
        ocean[l, rows : rows + 8, :] = jnp.zeros((8, cols), F32)
        for t in range(2):
            for s in (s0, s1):
                s[t * levels + l, 0:TOP, :] = jnp.zeros((TOP, cols), F32)
                s[t * levels + l, TOP + rows : TOP + rows + 8, :] = jnp.zeros((8, cols), F32)
        wn[0, l, 0:8, :] = jnp.zeros((8, cols), F32)
        wn[1, l, 0:8, :] = jnp.zeros((8, cols), F32)
        wn[2, l, 0:8, :] = jnp.zeros((8, cols), F32)
        return carry

    lax.fori_loop(0, levels, level_setup, 0)

    def row(s, r):
        return s[:, TOP + r : TOP + r + 1, :]

    def remote(src, dst, step, which, a, b):
        return pltpu.make_async_remote_copy(
            src_ref=src, dst_ref=dst, send_sem=send_sem.at[step, which],
            recv_sem=recv_sem.at[step, which], device_id=(a, b), device_id_type=MESH,
        )

    def to_east(step):
        return remote(se.at[step], rw.at[step], step, 0, lat, east)

    def to_west(step):
        return remote(sw.at[step], re.at[step], step, 1, lat, west)

    def to_north(step):
        return remote(sn.at[step], rs.at[step], step, 2, lat + 1, lon)

    def to_south(step):
        return remote(ss.at[step], rn.at[step], step, 3, lat - 1, lon)

    def to_fold(step, d):
        return pltpu.make_async_remote_copy(
            src_ref=sf.at[step], dst_ref=rf[step].at[lon], send_sem=fold_send.at[step, d - 1],
            recv_sem=fold_recv.at[step, d - 1], device_id=(lat, lax.rem(lon + d, nlon)),
            device_id_type=MESH,
        )

    def start_lat(step):
        @pl.when(jnp.logical_not(northern))
        def _():
            to_north(step).start()

        @pl.when(jnp.logical_not(southern))
        def _():
            to_south(step).start()

        @pl.when(northern)
        def _():
            for d in range(1, nlon):
                to_fold(step, d).start()

    def wait_lat(step):
        @pl.when(jnp.logical_not(northern))
        def _():
            to_north(step).wait_send()
            to_south(step).wait_recv()

        @pl.when(jnp.logical_not(southern))
        def _():
            to_south(step).wait_send()
            to_north(step).wait_recv()

        @pl.when(northern)
        def _():
            for d in range(1, nlon):
                to_fold(step, d).wait()

    def fill_rows(step, s):
        sn[step, 0:6] = row(s, rows - 2)
        sn[step, 6:12] = row(s, rows - 1)
        ss[step, 0:6] = row(s, 0)
        ss[step, 6:12] = row(s, 1)
        sf[step, 0:6] = row(s, rows - 1)
        sf[step, 6:12] = row(s, rows - 2)
        rf[step][lon] = sf[step]

    fill_rows(0, s0)
    sn[0, 12:15] = nc[:, rows - 1 : rows, :]
    sn[0, 15:18] = nk[:, rows - 1 : rows, :]
    sn[0, 18:21] = ocean[:, rows - 1 : rows, :]
    ss[0, 12:15] = ocean[:, 0:1, :]

    @pl.when(northern)
    def _():
        pl.semaphore_wait(barrier, nlon)

    @pl.when(southern)
    def _():
        pl.semaphore_wait(barrier, 3)

    @pl.when(jnp.logical_not(northern | southern))
    def _():
        pl.semaphore_wait(barrier, 4)

    start_lat(0)

    def pack(fields, target):
        for r in starts:
            acc = jnp.zeros((BLOCK, cols), F32)
            for k, (ref, index, base) in enumerate(fields):
                x = ref[index, base + r : base + r + BLOCK, :]
                acc = jnp.where(lane // 4 == k, pltpu.roll(x, (4 * k + 2) % cols, 1), acc)
            packed[r : r + BLOCK, :] = acc
        for h in range(rows // cols):
            target[h] = packed[h * cols : (h + 1) * cols, :].T

    halves = range(rows // cols)

    def column(ref, h, j, first, count):
        return ref[h, pl.ds(4 * first + j, count, stride=4), :]

    fields = [(s0, f, TOP) for f in range(2 * levels)]
    for ref in (ocean, ec, ek):
        fields += [(ref, l, 0) for l in range(levels)]
    pack(fields, t0)
    n = 2 * levels
    for h in halves:
        se[0, h, 0:n] = column(t0, h, 0, 0, n)
        se[0, h, n : 2 * n] = column(t0, h, 1, 0, n)
        for i in range(3):
            at = 2 * n + i * levels
            se[0, h, at : at + levels] = column(t0, h, 1, n + i * levels, levels)
        sw[0, h, 0:n] = column(t0, h, 2, 0, n)
        sw[0, h, n : 2 * n] = column(t0, h, 3, 0, n)
        sw[0, h, 2 * n : 2 * n + levels] = column(t0, h, 2, n, levels)
    to_east(0).start()
    to_west(0).start()

    def level_weights(l, carry):
        for r in starts:
            o = ocean[l, r : r + BLOCK, :]
            u = ec[l, r : r + BLOCK, :]
            opened = jnp.where(lane == cols - 1, 0.0, o * pltpu.roll(o, cols - 1, 1))
            ahead, center, forward, far = face_weights(u, ek[l, r : r + BLOCK, :], opened)
            outside = ((lane == 0) & ahead) | ((lane == cols - 2) & jnp.logical_not(ahead))
            we[0, l, r : r + BLOCK, :] = center
            we[1, l, r : r + BLOCK, :] = forward
            we[2, l, r : r + BLOCK, :] = jnp.where(outside, 0.0, far)
            u = nc[l, r : r + BLOCK, :]
            opened = o * ocean[l, r + 1 : r + 1 + BLOCK, :]
            ahead, center, forward, far = face_weights(u, nk[l, r : r + BLOCK, :], opened)
            wn[0, l, 8 + r : 8 + r + BLOCK, :] = center
            wn[1, l, 8 + r : 8 + r + BLOCK, :] = forward
            wn[2, l, 8 + r : 8 + r + BLOCK, :] = far
        return carry

    lax.fori_loop(0, levels, level_weights, 0)

    def advance(s, put):
        def level(l, carry):
            for r in starts:
                ea = we[0, l, r : r + BLOCK, :]
                eb = we[1, l, r : r + BLOCK, :]
                ee = we[2, l, r : r + BLOCK, :]
                na = wn[0, l, r : r + BLOCK + 8, :]
                nb = wn[1, l, r : r + BLOCK + 8, :]
                ne = wn[2, l, r : r + BLOCK + 8, :]
                o = ocean[l, r : r + BLOCK, :]
                for t in range(2):
                    f = t * levels + l
                    base = TOP + r
                    q = s[f, base : base + BLOCK, :]
                    far = jnp.where(ee <= 0.0, pltpu.roll(q, 1, 1), pltpu.roll(q, cols - 2, 1))
                    flux = ea * q + eb * pltpu.roll(q, cols - 1, 1) + ee * far
                    total = q - flux + pltpu.roll(flux, 1, 1)
                    b = s[f, base - 8 : base + BLOCK, :]
                    a = s[f, base - 9 : base + BLOCK - 1, :]
                    c = s[f, base - 7 : base + BLOCK + 1, :]
                    d = s[f, base - 6 : base + BLOCK + 2, :]
                    flux = na * b + nb * c + ne * jnp.where(ne <= 0.0, a, d)
                    total = total - flux[8:] + flux[7 : 7 + BLOCK]
                    put(t, l, r, o * total)
            return carry

        lax.fori_loop(0, levels, level, 0)

    def put_s1(t, l, r, value):
        s1[t * levels + l, TOP + r : TOP + r + BLOCK, :] = value

    def put_out(t, l, r, value):
        out[t, l, r : r + BLOCK, :] = value

    def rows_fixed(step, s, add):
        @pl.when(northern)
        def _():
            picked = rf[step][lax.div(fold_ref[0], jnp.int32(cols))]
            north_rows[...] = reversed_lanes(picked)

        @pl.when(jnp.logical_not(northern))
        def _():
            north_rows[...] = rn[step, 0:12]

        o0, o1 = ocean[:, 0:1, :], ocean[:, 1:2, :]
        oy, oz = ocean[:, rows - 2 : rows - 1, :], ocean[:, rows - 1 : rows, :]
        above = jnp.where(northern, oz, rn[0, 12:15])
        below = jnp.where(southern, 0.0, rs[0, 18:21])
        first = o0 * o1 * jnp.maximum(nc[:, 0:1, :], 0.0) * (-1.0 / 6.0)
        last = oy * oz * jnp.minimum(nc[:, rows - 2 : rows - 1, :], 0.0) * (-1.0 / 6.0)
        for t in range(2):
            part = slice(t * levels, (t + 1) * levels)
            part2 = slice((2 + t) * levels, (3 + t) * levels)
            q0, q1 = s[part, TOP : TOP + 1, :], s[part, TOP + 1 : TOP + 2, :]
            qy = s[part, TOP + rows - 2 : TOP + rows - 1, :]
            qz = s[part, TOP + rows - 1 : TOP + rows, :]
            m2 = jnp.where(southern, 0.0, rs[step, part])
            m1 = jnp.where(southern, 0.0, rs[step, part2])
            p0, p1 = north_rows[part], north_rows[part2]
            low = face_flux(
                m2, m1, q0, q1, jnp.where(southern, 0.0, rs[0, 12:15]),
                jnp.where(southern, 0.0, rs[0, 15:18]), below * o0,
            )
            high = face_flux(
                qy, qz, p0, p1, nc[:, rows - 1 : rows, :], nk[:, rows - 1 : rows, :], oz * above
            )
            enters = first * m1
            leaves = last * p0
            add(t, 0, o0 * (low - enters))
            add(t, 1, o1 * enters)
            add(t, rows - 2, -oy * leaves)
            add(t, rows - 1, oz * (leaves - high))

    def columns_fixed(step, tq):
        for h in halves:
            oy, oz, o0, o1 = [column(t0, h, j, n, levels) for j in range(4)]
            cy, cz, c0, _ = [column(t0, h, j, n + levels, levels) for j in range(4)]
            kz = column(t0, h, 1, n + 2 * levels, levels)
            om = rw[0, h, 2 * n : 2 * n + levels]
            cm = rw[0, h, 2 * n + levels : 2 * n + 2 * levels]
            km = rw[0, h, 2 * n + 2 * levels : 2 * n + 3 * levels]
            op = re[0, h, 2 * n : 2 * n + levels]
            first = o0 * o1 * jnp.maximum(c0, 0.0) * (-1.0 / 6.0)
            last = oy * oz * jnp.minimum(cy, 0.0) * (-1.0 / 6.0)
            for t in range(2):
                qy, qz, q0, q1 = [column(tq, h, j, t * levels, levels) for j in range(4)]
                m2 = rw[step, h, t * levels : (t + 1) * levels]
                m1 = rw[step, h, n + t * levels : n + (t + 1) * levels]
                p0 = re[step, h, t * levels : (t + 1) * levels]
                p1 = re[step, h, n + t * levels : n + (t + 1) * levels]
                low = face_flux(m2, m1, q0, q1, cm, km, om * o0)
                high = face_flux(qy, qz, p0, p1, cz, kz, oz * op)
                enters = first * m1
                leaves = last * p0
                for j, fix in enumerate(
                    (-oy * leaves, oz * (leaves - high), o0 * (low - enters), o1 * enters)
                ):
                    ct[h, pl.ds(4 * t * levels + j, levels, stride=4), :] = fix

    def spread_columns(add):
        edge = (lane < 2) | (lane >= cols - 2)
        for h in halves:
            ce[h * cols : (h + 1) * cols, :] = ct[h].T
        for r in starts:
            x = ce[r : r + BLOCK, :]
            for f in range(n):
                add(f, r, jnp.where(edge, pltpu.roll(x, (cols - 4 * f - 2) % cols, 1), 0.0))

    advance(s0, put_s1)
    for h in halves:
        ct[h] = jnp.zeros((cols, cols), F32)
    wait_lat(0)
    to_east(0).wait()
    to_west(0).wait()

    def add_row_s1(t, r, value):
        part = slice(t * levels, (t + 1) * levels)
        s1[part, TOP + r : TOP + r + 1, :] = s1[part, TOP + r : TOP + r + 1, :] + value

    rows_fixed(0, s0, add_row_s1)
    columns_fixed(0, t0)
    pack([(s1, f, TOP) for f in range(n)], t1)
    for h in halves:
        t1[h, 0 : 4 * n] = t1[h, 0 : 4 * n] + ct[h, 0 : 4 * n]
        se[1, h, 0:n] = column(t1, h, 0, 0, n)
        se[1, h, n : 2 * n] = column(t1, h, 1, 0, n)
        sw[1, h, 0:n] = column(t1, h, 2, 0, n)
        sw[1, h, n : 2 * n] = column(t1, h, 3, 0, n)
    to_east(1).start()
    to_west(1).start()

    def add_s1(f, r, value):
        at = slice(TOP + r, TOP + r + BLOCK)
        s1[f, at, :] = s1[f, at, :] + value

    spread_columns(add_s1)
    fill_rows(1, s1)
    start_lat(1)
    advance(s1, put_out)
    wait_lat(1)
    to_east(1).wait()
    to_west(1).wait()

    def add_row_out(t, r, value):
        out[t, :, r : r + 1, :] = out[t, :, r : r + 1, :] + value

    rows_fixed(1, s1, add_row_out)
    columns_fixed(1, t1)

    def add_out(f, r, value):
        t, l = divmod(f, levels)
        out[t, l, r : r + BLOCK, :] = out[t, l, r : r + BLOCK, :] + value

    spread_columns(add_out)


def local(tracers, east_courant, north_courant, east_kappa, north_kappa, ocean_mask, fold_map):
    nlat = lax.axis_size("lat")
    nlon = lax.axis_size("lon")
    levels, rows, cols = ocean_mask.shape
    fields = 2 * levels
    halves = rows // cols

    def scratch(*shape):
        return pltpu.VMEM(shape, F32)

    whole = pl.BlockSpec(memory_space=pltpu.VMEM)
    return pl.pallas_call(
        functools.partial(kernel, nlat, nlon),
        out_shape=jax.ShapeDtypeStruct(tracers.shape, F32),
        in_specs=[pl.BlockSpec(memory_space=pltpu.SMEM)] + [whole] * 6,
        out_specs=whole,
        scratch_shapes=[
            scratch(fields, TOP + rows + 8, cols),
            scratch(fields, TOP + rows + 8, cols),
            scratch(levels, rows + 8, cols),
            scratch(3, levels, rows, cols),
            scratch(3, levels, rows + 8, cols),
            scratch(rows, cols),
            scratch(halves, cols, cols),
            scratch(halves, cols, cols),
            scratch(halves, cols, cols),
            scratch(rows, cols),
            scratch(2, halves, 24, cols),
            scratch(2, halves, 16, cols),
            scratch(2, 21, 1, cols),
            scratch(2, 15, 1, cols),
            scratch(2, 12, 1, cols),
            scratch(2, halves, 16, cols),
            scratch(2, halves, 24, cols),
            scratch(2, 15, 1, cols),
            scratch(2, 21, 1, cols),
            scratch(nlon, 12, 1, cols),
            scratch(nlon, 12, 1, cols),
            scratch(12, 1, cols),
            pltpu.SemaphoreType.DMA((2, 4)),
            pltpu.SemaphoreType.DMA((2, 4)),
            pltpu.SemaphoreType.DMA((2, nlon - 1)),
            pltpu.SemaphoreType.DMA((2, nlon - 1)),
        ],
        compiler_params=pltpu.CompilerParams(
            collective_id=0, has_side_effects=True, vmem_limit_bytes=24 * 1024 * 1024
        ),
    )(fold_map, tracers, east_courant, north_courant, east_kappa, north_kappa, ocean_mask)


def solution(mesh):
    in_specs = (
        P(None, None, "lat", "lon"),
        P(None, "lat", "lon"),
        P(None, "lat", "lon"),
        P(None, "lat", "lon"),
        P(None, "lat", "lon"),
        P(None, "lat", "lon"),
        P("lon"),
    )
    out_specs = P(None, None, "lat", "lon")
    return jax.shard_map(local, mesh=mesh, in_specs=in_specs, out_specs=out_specs, check_vma=False)
```

```python
import functools

import jax
import jax.numpy as jnp
from jax import lax
from jax.experimental import pallas as pl
from jax.experimental.pallas import tpu as pltpu
from jax.sharding import PartitionSpec as P

MESH = pl.DeviceIdType.MESH
F32 = jnp.float32
TOP = 16
BLOCK = 32


def face_flux(behind, center, forward, beyond, courant, diffusivity, opened):
    centered = 7.0 * (center + forward) - (behind + beyond)
    upwind = 3.0 * (forward - center) - (beyond - behind)
    return opened * (
        courant * centered * (1.0 / 12.0)
        - jnp.abs(courant) * upwind * (1.0 / 12.0)
        - diffusivity * (forward - center)
    )


def face_weights(courant, diffusivity, opened):
    ahead = courant >= 0.0
    scaled = opened * courant * (1.0 / 6.0)
    spread = opened * diffusivity
    center = scaled * jnp.where(ahead, 5.0, 2.0) + spread
    forward = scaled * jnp.where(ahead, 2.0, 5.0) - spread
    return ahead, center, forward, -scaled


def reversed_lanes(values):
    lane = lax.broadcasted_iota(jnp.int32, values.shape, values.ndim - 1)
    axis = values.ndim - 1
    step = values.shape[-1] // 2
    while step:
        up = pltpu.roll(values, values.shape[-1] - step, axis)
        down = pltpu.roll(values, step, axis)
        values = jnp.where((lane & step) == 0, up, down)
        step //= 2
    return values


def kernel(
    nlat, nlon, fold_ref, tr_in, ec_in, nc_in, ek_in, nk_in, mask_in, result,
    tr, ec, nc, ek, nk, mask, out, flow, load_sem, store_sem,
    s0, s1, ocean, we, wn, packed, t0, t1, ct, ce,
    se, sw, sn, ss, sf, re, rw, rn, rs, rf0, rf1, north_rows,
    send_sem, recv_sem, fold_send, fold_recv,
):
    levels, rows, cols = mask.shape
    loads = {}
    for i, (name, src, dst) in enumerate(
        (
            ("tr", tr_in, tr), ("mask", mask_in, mask), ("nc", nc_in, nc),
            ("nk", nk_in, nk), ("ec", ec_in, ec), ("ek", ek_in, ek),
        )
    ):
        loads[name] = pltpu.make_async_copy(src, dst, load_sem.at[i])
        loads[name].start()
    lat = lax.axis_index("lat")
    lon = lax.axis_index("lon")
    southern = lat == 0
    northern = lat == nlat - 1
    east = lax.rem(lon + 1, nlon)
    west = lax.rem(lon + nlon - 1, nlon)
    barrier = pltpu.get_barrier_semaphore()
    rf = (rf0, rf1)

    def greet(a, b):
        pl.semaphore_signal(barrier, inc=1, device_id=(a, b), device_id_type=MESH)

    greet(lat, east)
    greet(lat, west)

    @pl.when(jnp.logical_not(southern))
    def _():
        greet(lat - 1, lon)

    @pl.when(jnp.logical_not(northern))
    def _():
        greet(lat + 1, lon)

    @pl.when(northern)
    def _():
        for d in range(2, nlon - 1):
            greet(lat, lax.rem(lon + d, nlon))

    lane = lax.broadcasted_iota(jnp.int32, (BLOCK, cols), 1)
    starts = range(0, rows, BLOCK)

    def level_setup(l, carry):
        for r in starts:
            o = mask[l, r : r + BLOCK, :].astype(F32)
            ocean[l, r : r + BLOCK, :] = o
            for t in range(2):
                s0[t * levels + l, TOP + r : TOP + r + BLOCK, :] = tr[t, l, r : r + BLOCK, :] * o
        ocean[l, rows : rows + 8, :] = jnp.zeros((8, cols), F32)
        for t in range(2):
            for s in (s0, s1):
                s[t * levels + l, 0:TOP, :] = jnp.zeros((TOP, cols), F32)
                s[t * levels + l, TOP + rows : TOP + rows + 8, :] = jnp.zeros((8, cols), F32)
        return carry

    loads["tr"].wait()
    loads["mask"].wait()
    lax.fori_loop(0, levels, level_setup, 0)
    for t in range(2):
        flow[t, 0:8, :] = jnp.zeros((8, cols), F32)
    loads["nc"].wait()
    loads["nk"].wait()

    def row(s, r):
        return s[:, TOP + r : TOP + r + 1, :]

    def remote(src, dst, step, which, a, b):
        return pltpu.make_async_remote_copy(
            src_ref=src, dst_ref=dst, send_sem=send_sem.at[step, which],
            recv_sem=recv_sem.at[step, which], device_id=(a, b), device_id_type=MESH,
        )

    def to_east(step):
        return remote(se.at[step], rw.at[step], step, 0, lat, east)

    def to_west(step):
        return remote(sw.at[step], re.at[step], step, 1, lat, west)

    def to_north(step):
        return remote(sn.at[step], rs.at[step], step, 2, lat + 1, lon)

    def to_south(step):
        return remote(ss.at[step], rn.at[step], step, 3, lat - 1, lon)

    def to_fold(step, d):
        return pltpu.make_async_remote_copy(
            src_ref=sf.at[step], dst_ref=rf[step].at[lon], send_sem=fold_send.at[step, d - 1],
            recv_sem=fold_recv.at[step, d - 1], device_id=(lat, lax.rem(lon + d, nlon)),
            device_id_type=MESH,
        )

    def start_lat(step):
        @pl.when(jnp.logical_not(northern))
        def _():
            to_north(step).start()

        @pl.when(jnp.logical_not(southern))
        def _():
            to_south(step).start()

        @pl.when(northern)
        def _():
            for d in range(1, nlon):
                to_fold(step, d).start()

    def wait_lat(step):
        @pl.when(jnp.logical_not(northern))
        def _():
            to_north(step).wait_send()
            to_south(step).wait_recv()

        @pl.when(jnp.logical_not(southern))
        def _():
            to_south(step).wait_send()
            to_north(step).wait_recv()

        @pl.when(northern)
        def _():
            for d in range(1, nlon):
                to_fold(step, d).wait()

    def fill_rows(step, s):
        sn[step, 0:6] = row(s, rows - 2)
        sn[step, 6:12] = row(s, rows - 1)
        ss[step, 0:6] = row(s, 0)
        ss[step, 6:12] = row(s, 1)
        sf[step, 0:6] = row(s, rows - 1)
        sf[step, 6:12] = row(s, rows - 2)
        rf[step][lon] = sf[step]

    fill_rows(0, s0)
    sn[0, 12:15] = nc[:, rows - 1 : rows, :]
    sn[0, 15:18] = nk[:, rows - 1 : rows, :]
    sn[0, 18:21] = ocean[:, rows - 1 : rows, :]
    ss[0, 12:15] = ocean[:, 0:1, :]

    @pl.when(northern)
    def _():
        pl.semaphore_wait(barrier, nlon)

    @pl.when(southern)
    def _():
        pl.semaphore_wait(barrier, 3)

    @pl.when(jnp.logical_not(northern | southern))
    def _():
        pl.semaphore_wait(barrier, 4)

    start_lat(0)

    loads["ec"].wait()
    loads["ek"].wait()

    def pack(fields, target):
        for r in starts:
            acc = jnp.zeros((BLOCK, cols), F32)
            for k, (ref, index, base) in enumerate(fields):
                x = ref[index, base + r : base + r + BLOCK, :]
                acc = jnp.where(lane // 4 == k, pltpu.roll(x, (4 * k + 2) % cols, 1), acc)
            packed[r : r + BLOCK, :] = acc
        for h in range(rows // cols):
            target[h] = packed[h * cols : (h + 1) * cols, :].T

    halves = range(rows // cols)

    def column(ref, h, j, first, count):
        return ref[h, pl.ds(4 * first + j, count, stride=4), :]

    fields = [(s0, f, TOP) for f in range(2 * levels)]
    for ref in (ocean, ec, ek):
        fields += [(ref, l, 0) for l in range(levels)]
    pack(fields, t0)
    n = 2 * levels
    for h in halves:
        se[0, h, 0:n] = column(t0, h, 0, 0, n)
        se[0, h, n : 2 * n] = column(t0, h, 1, 0, n)
        for i in range(3):
            at = 2 * n + i * levels
            se[0, h, at : at + levels] = column(t0, h, 1, n + i * levels, levels)
        sw[0, h, 0:n] = column(t0, h, 2, 0, n)
        sw[0, h, n : 2 * n] = column(t0, h, 3, 0, n)
        sw[0, h, 2 * n : 2 * n + levels] = column(t0, h, 2, n, levels)
    to_east(0).start()
    to_west(0).start()

    def level_weights(l, carry):
        for r in starts:
            o = ocean[l, r : r + BLOCK, :]
            u = ec[l, r : r + BLOCK, :]
            opened = jnp.where(lane == cols - 1, 0.0, o * pltpu.roll(o, cols - 1, 1))
            ahead, center, forward, far = face_weights(u, ek[l, r : r + BLOCK, :], opened)
            outside = ((lane == 0) & ahead) | ((lane == cols - 2) & jnp.logical_not(ahead))
            we[0, l, r : r + BLOCK, :] = center
            we[1, l, r : r + BLOCK, :] = forward
            we[2, l, r : r + BLOCK, :] = jnp.where(outside, 0.0, far)
            u = nc[l, r : r + BLOCK, :]
            opened = o * ocean[l, r + 1 : r + 1 + BLOCK, :]
            ahead, center, forward, far = face_weights(u, nk[l, r : r + BLOCK, :], opened)
            wn[0, l, r : r + BLOCK, :] = center
            wn[1, l, r : r + BLOCK, :] = forward
            wn[2, l, r : r + BLOCK, :] = far
        return carry

    lax.fori_loop(0, levels, level_weights, 0)

    def advance(s, put):
        def level(l, carry):
            for r in starts:
                ea = we[0, l, r : r + BLOCK, :]
                eb = we[1, l, r : r + BLOCK, :]
                ee = we[2, l, r : r + BLOCK, :]
                na = wn[0, l, r : r + BLOCK, :]
                nb = wn[1, l, r : r + BLOCK, :]
                ne = wn[2, l, r : r + BLOCK, :]
                o = ocean[l, r : r + BLOCK, :]
                for t in range(2):
                    f = t * levels + l
                    base = TOP + r
                    q = s[f, base : base + BLOCK, :]
                    far = jnp.where(ee <= 0.0, pltpu.roll(q, 1, 1), pltpu.roll(q, cols - 2, 1))
                    flux = ea * q + eb * pltpu.roll(q, cols - 1, 1) + ee * far
                    total = q - flux + pltpu.roll(flux, 1, 1)
                    a = s[f, base - 1 : base + BLOCK - 1, :]
                    c = s[f, base + 1 : base + BLOCK + 1, :]
                    d = s[f, base + 2 : base + BLOCK + 2, :]
                    flux = na * q + nb * c + ne * jnp.where(ne <= 0.0, a, d)
                    flow[t, 8 + r : 8 + r + BLOCK, :] = flux
                    total = total - flux + flow[t, 7 + r : 7 + r + BLOCK, :]
                    put(t, l, r, o * total)
            return carry

        lax.fori_loop(0, levels, level, 0)

    def put_s1(t, l, r, value):
        s1[t * levels + l, TOP + r : TOP + r + BLOCK, :] = value

    def put_out(t, l, r, value):
        out[t, l, r : r + BLOCK, :] = value

    def rows_fixed(step, s, add):
        @pl.when(northern)
        def _():
            picked = rf[step][lax.div(fold_ref[0], jnp.int32(cols))]
            north_rows[...] = reversed_lanes(picked)

        @pl.when(jnp.logical_not(northern))
        def _():
            north_rows[...] = rn[step, 0:12]

        o0, o1 = ocean[:, 0:1, :], ocean[:, 1:2, :]
        oy, oz = ocean[:, rows - 2 : rows - 1, :], ocean[:, rows - 1 : rows, :]
        above = jnp.where(northern, oz, rn[0, 12:15])
        below = jnp.where(southern, 0.0, rs[0, 18:21])
        first = o0 * o1 * jnp.maximum(nc[:, 0:1, :], 0.0) * (-1.0 / 6.0)
        last = oy * oz * jnp.minimum(nc[:, rows - 2 : rows - 1, :], 0.0) * (-1.0 / 6.0)
        for t in range(2):
            part = slice(t * levels, (t + 1) * levels)
            part2 = slice((2 + t) * levels, (3 + t) * levels)
            q0, q1 = s[part, TOP : TOP + 1, :], s[part, TOP + 1 : TOP + 2, :]
            qy = s[part, TOP + rows - 2 : TOP + rows - 1, :]
            qz = s[part, TOP + rows - 1 : TOP + rows, :]
            m2 = jnp.where(southern, 0.0, rs[step, part])
            m1 = jnp.where(southern, 0.0, rs[step, part2])
            p0, p1 = north_rows[part], north_rows[part2]
            low = face_flux(
                m2, m1, q0, q1, jnp.where(southern, 0.0, rs[0, 12:15]),
                jnp.where(southern, 0.0, rs[0, 15:18]), below * o0,
            )
            high = face_flux(
                qy, qz, p0, p1, nc[:, rows - 1 : rows, :], nk[:, rows - 1 : rows, :], oz * above
            )
            enters = first * m1
            leaves = last * p0
            add(t, 0, o0 * (low - enters))
            add(t, 1, o1 * enters)
            add(t, rows - 2, -oy * leaves)
            add(t, rows - 1, oz * (leaves - high))

    def columns_fixed(step, tq):
        for h in halves:
            oy, oz, o0, o1 = [column(t0, h, j, n, levels) for j in range(4)]
            cy, cz, c0, _ = [column(t0, h, j, n + levels, levels) for j in range(4)]
            kz = column(t0, h, 1, n + 2 * levels, levels)
            om = rw[0, h, 2 * n : 2 * n + levels]
            cm = rw[0, h, 2 * n + levels : 2 * n + 2 * levels]
            km = rw[0, h, 2 * n + 2 * levels : 2 * n + 3 * levels]
            op = re[0, h, 2 * n : 2 * n + levels]
            first = o0 * o1 * jnp.maximum(c0, 0.0) * (-1.0 / 6.0)
            last = oy * oz * jnp.minimum(cy, 0.0) * (-1.0 / 6.0)
            for t in range(2):
                qy, qz, q0, q1 = [column(tq, h, j, t * levels, levels) for j in range(4)]
                m2 = rw[step, h, t * levels : (t + 1) * levels]
                m1 = rw[step, h, n + t * levels : n + (t + 1) * levels]
                p0 = re[step, h, t * levels : (t + 1) * levels]
                p1 = re[step, h, n + t * levels : n + (t + 1) * levels]
                low = face_flux(m2, m1, q0, q1, cm, km, om * o0)
                high = face_flux(qy, qz, p0, p1, cz, kz, oz * op)
                enters = first * m1
                leaves = last * p0
                for j, fix in enumerate(
                    (-oy * leaves, oz * (leaves - high), o0 * (low - enters), o1 * enters)
                ):
                    ct[h, pl.ds(4 * t * levels + j, levels, stride=4), :] = fix

    def spread_columns(add, done):
        edge = (lane < 2) | (lane >= cols - 2)
        for h in halves:
            ce[h * cols : (h + 1) * cols, :] = ct[h].T
        for f in range(n):
            for r in starts:
                x = ce[r : r + BLOCK, :]
                add(f, r, jnp.where(edge, pltpu.roll(x, (cols - 4 * f - 2) % cols, 1), 0.0))
            done(f)

    advance(s0, put_s1)
    for h in halves:
        ct[h] = jnp.zeros((cols, cols), F32)
    wait_lat(0)
    to_east(0).wait()
    to_west(0).wait()

    def add_row_s1(t, r, value):
        part = slice(t * levels, (t + 1) * levels)
        s1[part, TOP + r : TOP + r + 1, :] = s1[part, TOP + r : TOP + r + 1, :] + value

    rows_fixed(0, s0, add_row_s1)
    columns_fixed(0, t0)
    pack([(s1, f, TOP) for f in range(n)], t1)
    for h in halves:
        t1[h, 0 : 4 * n] = t1[h, 0 : 4 * n] + ct[h, 0 : 4 * n]
        se[1, h, 0:n] = column(t1, h, 0, 0, n)
        se[1, h, n : 2 * n] = column(t1, h, 1, 0, n)
        sw[1, h, 0:n] = column(t1, h, 2, 0, n)
        sw[1, h, n : 2 * n] = column(t1, h, 3, 0, n)
    to_east(1).start()
    to_west(1).start()

    def add_s1(f, r, value):
        at = slice(TOP + r, TOP + r + BLOCK)
        s1[f, at, :] = s1[f, at, :] + value

    spread_columns(add_s1, lambda f: None)
    fill_rows(1, s1)
    start_lat(1)
    advance(s1, put_out)
    wait_lat(1)
    to_east(1).wait()
    to_west(1).wait()

    def add_row_out(t, r, value):
        out[t, :, r : r + 1, :] = out[t, :, r : r + 1, :] + value

    rows_fixed(1, s1, add_row_out)
    columns_fixed(1, t1)

    def add_out(f, r, value):
        t, l = divmod(f, levels)
        out[t, l, r : r + BLOCK, :] = out[t, l, r : r + BLOCK, :] + value

    def store(f):
        t, l = divmod(f, levels)
        return pltpu.make_async_copy(out.at[t, l], result.at[t, l], store_sem.at[f])

    spread_columns(add_out, lambda f: store(f).start())
    for f in range(n):
        store(f).wait()


def local(tracers, east_courant, north_courant, east_kappa, north_kappa, ocean_mask, fold_map):
    nlat = lax.axis_size("lat")
    nlon = lax.axis_size("lon")
    levels, rows, cols = ocean_mask.shape
    fields = 2 * levels
    halves = rows // cols

    def scratch(*shape):
        return pltpu.VMEM(shape, F32)

    return pl.pallas_call(
        functools.partial(kernel, nlat, nlon),
        out_shape=jax.ShapeDtypeStruct(tracers.shape, F32),
        in_specs=[pl.BlockSpec(memory_space=pltpu.SMEM)] + [pl.BlockSpec(memory_space=pltpu.HBM)] * 6,
        out_specs=pl.BlockSpec(memory_space=pltpu.HBM),
        scratch_shapes=[
            scratch(2, levels, rows, cols),
            scratch(levels, rows, cols),
            scratch(levels, rows, cols),
            scratch(levels, rows, cols),
            scratch(levels, rows, cols),
            pltpu.VMEM((levels, rows, cols), jnp.int32),
            scratch(2, levels, rows, cols),
            scratch(2, rows + 8, cols),
            pltpu.SemaphoreType.DMA((6,)),
            pltpu.SemaphoreType.DMA((fields,)),
            scratch(fields, TOP + rows + 8, cols),
            scratch(fields, TOP + rows + 8, cols),
            scratch(levels, rows + 8, cols),
            scratch(3, levels, rows, cols),
            scratch(3, levels, rows, cols),
            scratch(rows, cols),
            scratch(halves, cols, cols),
            scratch(halves, cols, cols),
            scratch(halves, cols, cols),
            scratch(rows, cols),
            scratch(2, halves, 24, cols),
            scratch(2, halves, 16, cols),
            scratch(2, 21, 1, cols),
            scratch(2, 15, 1, cols),
            scratch(2, 12, 1, cols),
            scratch(2, halves, 16, cols),
            scratch(2, halves, 24, cols),
            scratch(2, 15, 1, cols),
            scratch(2, 21, 1, cols),
            scratch(nlon, 12, 1, cols),
            scratch(nlon, 12, 1, cols),
            scratch(12, 1, cols),
            pltpu.SemaphoreType.DMA((2, 4)),
            pltpu.SemaphoreType.DMA((2, 4)),
            pltpu.SemaphoreType.DMA((2, nlon - 1)),
            pltpu.SemaphoreType.DMA((2, nlon - 1)),
        ],
        compiler_params=pltpu.CompilerParams(
            collective_id=0, has_side_effects=True, vmem_limit_bytes=58 * 1024 * 1024
        ),
    )(fold_map, tracers, east_courant, north_courant, east_kappa, north_kappa, ocean_mask)


def solution(mesh):
    in_specs = (
        P(None, None, "lat", "lon"),
        P(None, "lat", "lon"),
        P(None, "lat", "lon"),
        P(None, "lat", "lon"),
        P(None, "lat", "lon"),
        P(None, "lat", "lon"),
        P("lon"),
    )
    out_specs = P(None, None, "lat", "lon")
    return jax.shard_map(local, mesh=mesh, in_specs=in_specs, out_specs=out_specs, check_vma=False)
```

```python
import functools

import jax
import jax.numpy as jnp
from jax import lax
from jax.experimental import pallas as pl
from jax.experimental.pallas import tpu as pltpu
from jax.sharding import PartitionSpec as P

MESH = pl.DeviceIdType.MESH
F32 = jnp.float32
TOP = 16
BLOCK = 32


def face_flux(behind, center, forward, beyond, courant, diffusivity, opened):
    centered = 7.0 * (center + forward) - (behind + beyond)
    upwind = 3.0 * (forward - center) - (beyond - behind)
    return opened * (
        courant * centered * (1.0 / 12.0)
        - jnp.abs(courant) * upwind * (1.0 / 12.0)
        - diffusivity * (forward - center)
    )


def face_weights(courant, diffusivity, opened):
    ahead = courant >= 0.0
    scaled = opened * courant * (1.0 / 6.0)
    spread = opened * diffusivity
    center = scaled * jnp.where(ahead, 5.0, 2.0) + spread
    forward = scaled * jnp.where(ahead, 2.0, 5.0) - spread
    return ahead, center, forward, -scaled


def reversed_lanes(values):
    lane = lax.broadcasted_iota(jnp.int32, values.shape, values.ndim - 1)
    axis = values.ndim - 1
    step = values.shape[-1] // 2
    while step:
        up = pltpu.roll(values, values.shape[-1] - step, axis)
        down = pltpu.roll(values, step, axis)
        values = jnp.where((lane & step) == 0, up, down)
        step //= 2
    return values


def kernel(
    nlat, nlon, fold_ref, tr_in, ec_in, nc_in, ek_in, nk_in, mask_in, out,
    tr, ec, nc, ek, nk, mask, flow, load_sem,
    s0, s1, ocean, we, wn, packed, t0, t1, ct, ce,
    se, sw, sn, ss, sf, re, rw, rn, rs, rf0, rf1, north_rows,
    send_sem, recv_sem, fold_send, fold_recv,
):
    levels, rows, cols = mask.shape
    loads = {}
    for i, (name, src, dst) in enumerate(
        (
            ("tr", tr_in, tr), ("mask", mask_in, mask), ("nc", nc_in, nc),
            ("nk", nk_in, nk), ("ec", ec_in, ec), ("ek", ek_in, ek),
        )
    ):
        loads[name] = pltpu.make_async_copy(src, dst, load_sem.at[i])
        loads[name].start()
    lat = lax.axis_index("lat")
    lon = lax.axis_index("lon")
    southern = lat == 0
    northern = lat == nlat - 1
    east = lax.rem(lon + 1, nlon)
    west = lax.rem(lon + nlon - 1, nlon)
    barrier = pltpu.get_barrier_semaphore()
    rf = (rf0, rf1)

    def greet(a, b):
        pl.semaphore_signal(barrier, inc=1, device_id=(a, b), device_id_type=MESH)

    greet(lat, east)
    greet(lat, west)

    @pl.when(jnp.logical_not(southern))
    def _():
        greet(lat - 1, lon)

    @pl.when(jnp.logical_not(northern))
    def _():
        greet(lat + 1, lon)

    @pl.when(northern)
    def _():
        for d in range(2, nlon - 1):
            greet(lat, lax.rem(lon + d, nlon))

    lane = lax.broadcasted_iota(jnp.int32, (BLOCK, cols), 1)
    starts = range(0, rows, BLOCK)

    def level_setup(l, carry):
        for r in starts:
            o = mask[l, r : r + BLOCK, :].astype(F32)
            ocean[l, r : r + BLOCK, :] = o
            for t in range(2):
                s0[t * levels + l, TOP + r : TOP + r + BLOCK, :] = tr[t, l, r : r + BLOCK, :] * o
        ocean[l, rows : rows + 8, :] = jnp.zeros((8, cols), F32)
        for t in range(2):
            for s in (s0, s1):
                s[t * levels + l, 0:TOP, :] = jnp.zeros((TOP, cols), F32)
                s[t * levels + l, TOP + rows : TOP + rows + 8, :] = jnp.zeros((8, cols), F32)
        return carry

    loads["tr"].wait()
    loads["mask"].wait()
    lax.fori_loop(0, levels, level_setup, 0)
    for t in range(2):
        flow[t, 0:8, :] = jnp.zeros((8, cols), F32)
    loads["nc"].wait()
    loads["nk"].wait()

    def row(s, r):
        return s[:, TOP + r : TOP + r + 1, :]

    def remote(src, dst, step, which, a, b):
        return pltpu.make_async_remote_copy(
            src_ref=src, dst_ref=dst, send_sem=send_sem.at[step, which],
            recv_sem=recv_sem.at[step, which], device_id=(a, b), device_id_type=MESH,
        )

    def to_east(step):
        return remote(se.at[step], rw.at[step], step, 0, lat, east)

    def to_west(step):
        return remote(sw.at[step], re.at[step], step, 1, lat, west)

    def to_north(step):
        return remote(sn.at[step], rs.at[step], step, 2, lat + 1, lon)

    def to_south(step):
        return remote(ss.at[step], rn.at[step], step, 3, lat - 1, lon)

    def to_fold(step, d):
        return pltpu.make_async_remote_copy(
            src_ref=sf.at[step], dst_ref=rf[step].at[lon], send_sem=fold_send.at[step, d - 1],
            recv_sem=fold_recv.at[step, d - 1], device_id=(lat, lax.rem(lon + d, nlon)),
            device_id_type=MESH,
        )

    def start_lat(step):
        @pl.when(jnp.logical_not(northern))
        def _():
            to_north(step).start()

        @pl.when(jnp.logical_not(southern))
        def _():
            to_south(step).start()

        @pl.when(northern)
        def _():
            for d in range(1, nlon):
                to_fold(step, d).start()

    def wait_lat(step):
        @pl.when(jnp.logical_not(northern))
        def _():
            to_north(step).wait_send()
            to_south(step).wait_recv()

        @pl.when(jnp.logical_not(southern))
        def _():
            to_south(step).wait_send()
            to_north(step).wait_recv()

        @pl.when(northern)
        def _():
            for d in range(1, nlon):
                to_fold(step, d).wait()

    def fill_rows(step, s):
        sn[step, 0:6] = row(s, rows - 2)
        sn[step, 6:12] = row(s, rows - 1)
        ss[step, 0:6] = row(s, 0)
        ss[step, 6:12] = row(s, 1)
        sf[step, 0:6] = row(s, rows - 1)
        sf[step, 6:12] = row(s, rows - 2)
        rf[step][lon] = sf[step]

    fill_rows(0, s0)
    sn[0, 12:15] = nc[:, rows - 1 : rows, :]
    sn[0, 15:18] = nk[:, rows - 1 : rows, :]
    sn[0, 18:21] = ocean[:, rows - 1 : rows, :]
    ss[0, 12:15] = ocean[:, 0:1, :]

    @pl.when(northern)
    def _():
        pl.semaphore_wait(barrier, nlon)

    @pl.when(southern)
    def _():
        pl.semaphore_wait(barrier, 3)

    @pl.when(jnp.logical_not(northern | southern))
    def _():
        pl.semaphore_wait(barrier, 4)

    start_lat(0)

    loads["ec"].wait()
    loads["ek"].wait()

    def pack(fields, target):
        for r in starts:
            acc = jnp.zeros((BLOCK, cols), F32)
            for k, (ref, index, base) in enumerate(fields):
                x = ref[index, base + r : base + r + BLOCK, :]
                acc = jnp.where(lane // 4 == k, pltpu.roll(x, (4 * k + 2) % cols, 1), acc)
            packed[r : r + BLOCK, :] = acc
        for h in range(rows // cols):
            target[h] = packed[h * cols : (h + 1) * cols, :].T

    halves = range(rows // cols)

    def column(ref, h, j, first, count):
        return ref[h, pl.ds(4 * first + j, count, stride=4), :]

    fields = [(s0, f, TOP) for f in range(2 * levels)]
    for ref in (ocean, ec, ek):
        fields += [(ref, l, 0) for l in range(levels)]
    pack(fields, t0)
    n = 2 * levels
    for h in halves:
        se[0, h, 0:n] = column(t0, h, 0, 0, n)
        se[0, h, n : 2 * n] = column(t0, h, 1, 0, n)
        for i in range(3):
            at = 2 * n + i * levels
            se[0, h, at : at + levels] = column(t0, h, 1, n + i * levels, levels)
        sw[0, h, 0:n] = column(t0, h, 2, 0, n)
        sw[0, h, n : 2 * n] = column(t0, h, 3, 0, n)
        sw[0, h, 2 * n : 2 * n + levels] = column(t0, h, 2, n, levels)
    to_east(0).start()
    to_west(0).start()

    def level_weights(l, carry):
        for r in starts:
            o = ocean[l, r : r + BLOCK, :]
            u = ec[l, r : r + BLOCK, :]
            opened = jnp.where(lane == cols - 1, 0.0, o * pltpu.roll(o, cols - 1, 1))
            ahead, center, forward, far = face_weights(u, ek[l, r : r + BLOCK, :], opened)
            outside = ((lane == 0) & ahead) | ((lane == cols - 2) & jnp.logical_not(ahead))
            we[0, l, r : r + BLOCK, :] = center
            we[1, l, r : r + BLOCK, :] = forward
            we[2, l, r : r + BLOCK, :] = jnp.where(outside, 0.0, far)
            u = nc[l, r : r + BLOCK, :]
            opened = o * ocean[l, r + 1 : r + 1 + BLOCK, :]
            ahead, center, forward, far = face_weights(u, nk[l, r : r + BLOCK, :], opened)
            wn[0, l, r : r + BLOCK, :] = center
            wn[1, l, r : r + BLOCK, :] = forward
            wn[2, l, r : r + BLOCK, :] = far
        return carry

    lax.fori_loop(0, levels, level_weights, 0)

    def advance(s, put):
        def level(l, carry):
            for r in starts:
                ea = we[0, l, r : r + BLOCK, :]
                eb = we[1, l, r : r + BLOCK, :]
                ee = we[2, l, r : r + BLOCK, :]
                na = wn[0, l, r : r + BLOCK, :]
                nb = wn[1, l, r : r + BLOCK, :]
                ne = wn[2, l, r : r + BLOCK, :]
                o = ocean[l, r : r + BLOCK, :]
                for t in range(2):
                    f = t * levels + l
                    base = TOP + r
                    q = s[f, base : base + BLOCK, :]
                    far = jnp.where(ee <= 0.0, pltpu.roll(q, 1, 1), pltpu.roll(q, cols - 2, 1))
                    flux = ea * q + eb * pltpu.roll(q, cols - 1, 1) + ee * far
                    total = q - flux + pltpu.roll(flux, 1, 1)
                    a = s[f, base - 1 : base + BLOCK - 1, :]
                    c = s[f, base + 1 : base + BLOCK + 1, :]
                    d = s[f, base + 2 : base + BLOCK + 2, :]
                    flux = na * q + nb * c + ne * jnp.where(ne <= 0.0, a, d)
                    flow[t, 8 + r : 8 + r + BLOCK, :] = flux
                    total = total - flux + flow[t, 7 + r : 7 + r + BLOCK, :]
                    put(t, l, r, o * total)
            return carry

        lax.fori_loop(0, levels, level, 0)

    def put_s1(t, l, r, value):
        s1[t * levels + l, TOP + r : TOP + r + BLOCK, :] = value

    def put_out(t, l, r, value):
        out[t, l, r : r + BLOCK, :] = value

    def rows_fixed(step, s, add):
        @pl.when(northern)
        def _():
            picked = rf[step][lax.div(fold_ref[0], jnp.int32(cols))]
            north_rows[...] = reversed_lanes(picked)

        @pl.when(jnp.logical_not(northern))
        def _():
            north_rows[...] = rn[step, 0:12]

        o0, o1 = ocean[:, 0:1, :], ocean[:, 1:2, :]
        oy, oz = ocean[:, rows - 2 : rows - 1, :], ocean[:, rows - 1 : rows, :]
        above = jnp.where(northern, oz, rn[0, 12:15])
        below = jnp.where(southern, 0.0, rs[0, 18:21])
        first = o0 * o1 * jnp.maximum(nc[:, 0:1, :], 0.0) * (-1.0 / 6.0)
        last = oy * oz * jnp.minimum(nc[:, rows - 2 : rows - 1, :], 0.0) * (-1.0 / 6.0)
        for t in range(2):
            part = slice(t * levels, (t + 1) * levels)
            part2 = slice((2 + t) * levels, (3 + t) * levels)
            q0, q1 = s[part, TOP : TOP + 1, :], s[part, TOP + 1 : TOP + 2, :]
            qy = s[part, TOP + rows - 2 : TOP + rows - 1, :]
            qz = s[part, TOP + rows - 1 : TOP + rows, :]
            m2 = jnp.where(southern, 0.0, rs[step, part])
            m1 = jnp.where(southern, 0.0, rs[step, part2])
            p0, p1 = north_rows[part], north_rows[part2]
            low = face_flux(
                m2, m1, q0, q1, jnp.where(southern, 0.0, rs[0, 12:15]),
                jnp.where(southern, 0.0, rs[0, 15:18]), below * o0,
            )
            high = face_flux(
                qy, qz, p0, p1, nc[:, rows - 1 : rows, :], nk[:, rows - 1 : rows, :], oz * above
            )
            enters = first * m1
            leaves = last * p0
            add(t, 0, o0 * (low - enters))
            add(t, 1, o1 * enters)
            add(t, rows - 2, -oy * leaves)
            add(t, rows - 1, oz * (leaves - high))

    def columns_fixed(step, tq):
        for h in halves:
            oy, oz, o0, o1 = [column(t0, h, j, n, levels) for j in range(4)]
            cy, cz, c0, _ = [column(t0, h, j, n + levels, levels) for j in range(4)]
            kz = column(t0, h, 1, n + 2 * levels, levels)
            om = rw[0, h, 2 * n : 2 * n + levels]
            cm = rw[0, h, 2 * n + levels : 2 * n + 2 * levels]
            km = rw[0, h, 2 * n + 2 * levels : 2 * n + 3 * levels]
            op = re[0, h, 2 * n : 2 * n + levels]
            first = o0 * o1 * jnp.maximum(c0, 0.0) * (-1.0 / 6.0)
            last = oy * oz * jnp.minimum(cy, 0.0) * (-1.0 / 6.0)
            for t in range(2):
                qy, qz, q0, q1 = [column(tq, h, j, t * levels, levels) for j in range(4)]
                m2 = rw[step, h, t * levels : (t + 1) * levels]
                m1 = rw[step, h, n + t * levels : n + (t + 1) * levels]
                p0 = re[step, h, t * levels : (t + 1) * levels]
                p1 = re[step, h, n + t * levels : n + (t + 1) * levels]
                low = face_flux(m2, m1, q0, q1, cm, km, om * o0)
                high = face_flux(qy, qz, p0, p1, cz, kz, oz * op)
                enters = first * m1
                leaves = last * p0
                for j, fix in enumerate(
                    (-oy * leaves, oz * (leaves - high), o0 * (low - enters), o1 * enters)
                ):
                    ct[h, pl.ds(4 * t * levels + j, levels, stride=4), :] = fix

    def turn_columns():
        for h in halves:
            ce[h * cols : (h + 1) * cols, :] = ct[h].T

    def spread_columns(add, blocks):
        edge = (lane < 2) | (lane >= cols - 2)
        for f in range(n):
            for r in blocks:
                x = ce[r : r + BLOCK, :]
                add(f, r, jnp.where(edge, pltpu.roll(x, (cols - 4 * f - 2) % cols, 1), 0.0))

    advance(s0, put_s1)
    for h in halves:
        ct[h] = jnp.zeros((cols, cols), F32)
    wait_lat(0)
    to_east(0).wait()
    to_west(0).wait()

    def add_row_s1(t, r, value):
        part = slice(t * levels, (t + 1) * levels)
        s1[part, TOP + r : TOP + r + 1, :] = s1[part, TOP + r : TOP + r + 1, :] + value

    rows_fixed(0, s0, add_row_s1)
    columns_fixed(0, t0)
    pack([(s1, f, TOP) for f in range(n)], t1)
    for h in halves:
        t1[h, 0 : 4 * n] = t1[h, 0 : 4 * n] + ct[h, 0 : 4 * n]
        se[1, h, 0:n] = column(t1, h, 0, 0, n)
        se[1, h, n : 2 * n] = column(t1, h, 1, 0, n)
        sw[1, h, 0:n] = column(t1, h, 2, 0, n)
        sw[1, h, n : 2 * n] = column(t1, h, 3, 0, n)
    to_east(1).start()
    to_west(1).start()

    def add_s1(f, r, value):
        at = slice(TOP + r, TOP + r + BLOCK)
        s1[f, at, :] = s1[f, at, :] + value

    turn_columns()
    spread_columns(add_s1, (starts[0], starts[-1]))
    fill_rows(1, s1)
    start_lat(1)
    spread_columns(add_s1, starts[1:-1])
    advance(s1, put_out)
    wait_lat(1)
    to_east(1).wait()
    to_west(1).wait()

    def add_row_out(t, r, value):
        out[t, :, r : r + 1, :] = out[t, :, r : r + 1, :] + value

    rows_fixed(1, s1, add_row_out)
    columns_fixed(1, t1)

    def add_out(f, r, value):
        t, l = divmod(f, levels)
        out[t, l, r : r + BLOCK, :] = out[t, l, r : r + BLOCK, :] + value

    turn_columns()
    spread_columns(add_out, starts)


def local(tracers, east_courant, north_courant, east_kappa, north_kappa, ocean_mask, fold_map):
    nlat = lax.axis_size("lat")
    nlon = lax.axis_size("lon")
    levels, rows, cols = ocean_mask.shape
    fields = 2 * levels
    halves = rows // cols

    def scratch(*shape):
        return pltpu.VMEM(shape, F32)

    return pl.pallas_call(
        functools.partial(kernel, nlat, nlon),
        out_shape=pltpu.VMEM(tracers.shape, F32),
        in_specs=[pl.BlockSpec(memory_space=pltpu.SMEM)] + [pl.BlockSpec(memory_space=pltpu.HBM)] * 6,
        out_specs=pl.BlockSpec(memory_space=pltpu.VMEM),
        scratch_shapes=[
            scratch(2, levels, rows, cols),
            scratch(levels, rows, cols),
            scratch(levels, rows, cols),
            scratch(levels, rows, cols),
            scratch(levels, rows, cols),
            pltpu.VMEM((levels, rows, cols), jnp.int32),
            scratch(2, rows + 8, cols),
            pltpu.SemaphoreType.DMA((6,)),
            scratch(fields, TOP + rows + 8, cols),
            scratch(fields, TOP + rows + 8, cols),
            scratch(levels, rows + 8, cols),
            scratch(3, levels, rows, cols),
            scratch(3, levels, rows, cols),
            scratch(rows, cols),
            scratch(halves, cols, cols),
            scratch(halves, cols, cols),
            scratch(halves, cols, cols),
            scratch(rows, cols),
            scratch(2, halves, 24, cols),
            scratch(2, halves, 16, cols),
            scratch(2, 21, 1, cols),
            scratch(2, 15, 1, cols),
            scratch(2, 12, 1, cols),
            scratch(2, halves, 16, cols),
            scratch(2, halves, 24, cols),
            scratch(2, 15, 1, cols),
            scratch(2, 21, 1, cols),
            scratch(nlon, 12, 1, cols),
            scratch(nlon, 12, 1, cols),
            scratch(12, 1, cols),
            pltpu.SemaphoreType.DMA((2, 4)),
            pltpu.SemaphoreType.DMA((2, 4)),
            pltpu.SemaphoreType.DMA((2, nlon - 1)),
            pltpu.SemaphoreType.DMA((2, nlon - 1)),
        ],
        compiler_params=pltpu.CompilerParams(
            collective_id=0, has_side_effects=True, vmem_limit_bytes=55 * 1024 * 1024
        ),
    )(
        fold_map,
        *(
            pltpu.with_memory_space_constraint(x, pltpu.HBM)
            for x in (tracers, east_courant, north_courant, east_kappa, north_kappa, ocean_mask)
        ),
    )


def solution(mesh):
    in_specs = (
        P(None, None, "lat", "lon"),
        P(None, "lat", "lon"),
        P(None, "lat", "lon"),
        P(None, "lat", "lon"),
        P(None, "lat", "lon"),
        P(None, "lat", "lon"),
        P("lon"),
    )
    out_specs = P(None, None, "lat", "lon")
    return jax.shard_map(local, mesh=mesh, in_specs=in_specs, out_specs=out_specs, check_vma=False)
```

```python
import functools

import jax
import jax.numpy as jnp
from jax import lax
from jax.experimental import pallas as pl
from jax.experimental.pallas import tpu as pltpu
from jax.sharding import PartitionSpec as P

MESH = pl.DeviceIdType.MESH
F32 = jnp.float32
TOP = 16
BLOCK = 16


def face_flux(behind, center, forward, beyond, courant, diffusivity, opened):
    centered = 7.0 * (center + forward) - (behind + beyond)
    upwind = 3.0 * (forward - center) - (beyond - behind)
    return opened * (
        courant * centered * (1.0 / 12.0)
        - jnp.abs(courant) * upwind * (1.0 / 12.0)
        - diffusivity * (forward - center)
    )


def face_weights(courant, diffusivity, opened):
    ahead = courant >= 0.0
    scaled = opened * courant * (1.0 / 6.0)
    spread = opened * diffusivity
    center = scaled * jnp.where(ahead, 5.0, 2.0) + spread
    forward = scaled * jnp.where(ahead, 2.0, 5.0) - spread
    return ahead, center, forward, -scaled


def reversed_lanes(values):
    lane = lax.broadcasted_iota(jnp.int32, values.shape, values.ndim - 1)
    axis = values.ndim - 1
    step = values.shape[-1] // 2
    while step:
        up = pltpu.roll(values, values.shape[-1] - step, axis)
        down = pltpu.roll(values, step, axis)
        values = jnp.where((lane & step) == 0, up, down)
        step //= 2
    return values


def kernel(
    nlat, nlon, fold_ref, tr_in, ec_in, nc_in, ek_in, nk_in, mask_in, out,
    tr, ec, nc, ek, nk, mask, flow, load_sem,
    s0, s1, ocean, we, wn, packed, t0, t1, ct, ce,
    se, sw, sn, ss, sf, re, rw, rn, rs, rf0, rf1, north_rows,
    send_sem, recv_sem, fold_send, fold_recv,
):
    levels, rows, cols = mask.shape
    loads = {}
    for i, (name, src, dst) in enumerate(
        (
            ("tr", tr_in, tr), ("mask", mask_in, mask), ("nc", nc_in, nc),
            ("nk", nk_in, nk), ("ec", ec_in, ec), ("ek", ek_in, ek),
        )
    ):
        loads[name] = pltpu.make_async_copy(src, dst, load_sem.at[i])
        loads[name].start()
    lat = lax.axis_index("lat")
    lon = lax.axis_index("lon")
    southern = lat == 0
    northern = lat == nlat - 1
    east = lax.rem(lon + 1, nlon)
    west = lax.rem(lon + nlon - 1, nlon)
    barrier = pltpu.get_barrier_semaphore()
    rf = (rf0, rf1)

    def greet(a, b):
        pl.semaphore_signal(barrier, inc=1, device_id=(a, b), device_id_type=MESH)

    greet(lat, east)
    greet(lat, west)

    @pl.when(jnp.logical_not(southern))
    def _():
        greet(lat - 1, lon)

    @pl.when(jnp.logical_not(northern))
    def _():
        greet(lat + 1, lon)

    @pl.when(northern)
    def _():
        for d in range(2, nlon - 1):
            greet(lat, lax.rem(lon + d, nlon))

    lane = lax.broadcasted_iota(jnp.int32, (BLOCK, cols), 1)
    starts = range(0, rows, BLOCK)

    def level_setup(l, carry):
        for r in starts:
            o = mask[l, r : r + BLOCK, :].astype(F32)
            ocean[l, r : r + BLOCK, :] = o
            for t in range(2):
                s0[t * levels + l, TOP + r : TOP + r + BLOCK, :] = tr[t, l, r : r + BLOCK, :] * o
        ocean[l, rows : rows + 8, :] = jnp.zeros((8, cols), F32)
        for t in range(2):
            for s in (s0, s1):
                s[t * levels + l, 0:TOP, :] = jnp.zeros((TOP, cols), F32)
                s[t * levels + l, TOP + rows : TOP + rows + 8, :] = jnp.zeros((8, cols), F32)
        return carry

    loads["tr"].wait()
    loads["mask"].wait()
    lax.fori_loop(0, levels, level_setup, 0)
    for t in range(2):
        flow[t, 0:8, :] = jnp.zeros((8, cols), F32)
    loads["nc"].wait()
    loads["nk"].wait()

    def row(s, r):
        return s[:, TOP + r : TOP + r + 1, :]

    def remote(src, dst, step, which, a, b):
        return pltpu.make_async_remote_copy(
            src_ref=src, dst_ref=dst, send_sem=send_sem.at[step, which],
            recv_sem=recv_sem.at[step, which], device_id=(a, b), device_id_type=MESH,
        )

    def to_east(step):
        return remote(se.at[step], rw.at[step], step, 0, lat, east)

    def to_west(step):
        return remote(sw.at[step], re.at[step], step, 1, lat, west)

    def to_north(step):
        return remote(sn.at[step], rs.at[step], step, 2, lat + 1, lon)

    def to_south(step):
        return remote(ss.at[step], rn.at[step], step, 3, lat - 1, lon)

    def to_fold(step, d):
        return pltpu.make_async_remote_copy(
            src_ref=sf.at[step], dst_ref=rf[step].at[lon], send_sem=fold_send.at[step, d - 1],
            recv_sem=fold_recv.at[step, d - 1], device_id=(lat, lax.rem(lon + d, nlon)),
            device_id_type=MESH,
        )

    def start_lat(step):
        @pl.when(jnp.logical_not(northern))
        def _():
            to_north(step).start()

        @pl.when(jnp.logical_not(southern))
        def _():
            to_south(step).start()

        @pl.when(northern)
        def _():
            for d in range(1, nlon):
                to_fold(step, d).start()

    def wait_lat(step):
        @pl.when(jnp.logical_not(northern))
        def _():
            to_north(step).wait_send()
            to_south(step).wait_recv()

        @pl.when(jnp.logical_not(southern))
        def _():
            to_south(step).wait_send()
            to_north(step).wait_recv()

        @pl.when(northern)
        def _():
            for d in range(1, nlon):
                to_fold(step, d).wait()

    def fill_rows(step, s):
        sn[step, 0:6] = row(s, rows - 2)
        sn[step, 6:12] = row(s, rows - 1)
        ss[step, 0:6] = row(s, 0)
        ss[step, 6:12] = row(s, 1)
        sf[step, 0:6] = row(s, rows - 1)
        sf[step, 6:12] = row(s, rows - 2)
        rf[step][lon] = sf[step]

    fill_rows(0, s0)
    sn[0, 12:15] = nc[:, rows - 1 : rows, :]
    sn[0, 15:18] = nk[:, rows - 1 : rows, :]
    sn[0, 18:21] = ocean[:, rows - 1 : rows, :]
    ss[0, 12:15] = ocean[:, 0:1, :]

    @pl.when(northern)
    def _():
        pl.semaphore_wait(barrier, nlon)

    @pl.when(southern)
    def _():
        pl.semaphore_wait(barrier, 3)

    @pl.when(jnp.logical_not(northern | southern))
    def _():
        pl.semaphore_wait(barrier, 4)

    start_lat(0)

    loads["ec"].wait()
    loads["ek"].wait()

    def pack(fields, target):
        for r in starts:
            acc = jnp.zeros((BLOCK, cols), F32)
            for k, (ref, index, base) in enumerate(fields):
                x = ref[index, base + r : base + r + BLOCK, :]
                acc = jnp.where(lane // 4 == k, pltpu.roll(x, (4 * k + 2) % cols, 1), acc)
            packed[r : r + BLOCK, :] = acc
        for h in range(rows // cols):
            target[h] = packed[h * cols : (h + 1) * cols, :].T

    halves = range(rows // cols)

    def column(ref, h, j, first, count):
        return ref[h, pl.ds(4 * first + j, count, stride=4), :]

    fields = [(s0, f, TOP) for f in range(2 * levels)]
    for ref in (ocean, ec, ek):
        fields += [(ref, l, 0) for l in range(levels)]
    pack(fields, t0)
    n = 2 * levels
    for h in halves:
        se[0, h, 0:n] = column(t0, h, 0, 0, n)
        se[0, h, n : 2 * n] = column(t0, h, 1, 0, n)
        for i in range(3):
            at = 2 * n + i * levels
            se[0, h, at : at + levels] = column(t0, h, 1, n + i * levels, levels)
        sw[0, h, 0:n] = column(t0, h, 2, 0, n)
        sw[0, h, n : 2 * n] = column(t0, h, 3, 0, n)
        sw[0, h, 2 * n : 2 * n + levels] = column(t0, h, 2, n, levels)
    to_east(0).start()
    to_west(0).start()

    def level_weights(l, carry):
        for r in starts:
            o = ocean[l, r : r + BLOCK, :]
            u = ec[l, r : r + BLOCK, :]
            opened = jnp.where(lane == cols - 1, 0.0, o * pltpu.roll(o, cols - 1, 1))
            ahead, center, forward, far = face_weights(u, ek[l, r : r + BLOCK, :], opened)
            outside = ((lane == 0) & ahead) | ((lane == cols - 2) & jnp.logical_not(ahead))
            we[0, l, r : r + BLOCK, :] = center
            we[1, l, r : r + BLOCK, :] = forward
            we[2, l, r : r + BLOCK, :] = jnp.where(outside, 0.0, far)
            u = nc[l, r : r + BLOCK, :]
            opened = o * ocean[l, r + 1 : r + 1 + BLOCK, :]
            ahead, center, forward, far = face_weights(u, nk[l, r : r + BLOCK, :], opened)
            wn[0, l, r : r + BLOCK, :] = center
            wn[1, l, r : r + BLOCK, :] = forward
            wn[2, l, r : r + BLOCK, :] = far
        return carry

    lax.fori_loop(0, levels, level_weights, 0)

    def advance(s, put):
        def level(l, carry):
            for r in starts:
                ea = we[0, l, r : r + BLOCK, :]
                eb = we[1, l, r : r + BLOCK, :]
                ee = we[2, l, r : r + BLOCK, :]
                na = wn[0, l, r : r + BLOCK, :]
                nb = wn[1, l, r : r + BLOCK, :]
                ne = wn[2, l, r : r + BLOCK, :]
                o = ocean[l, r : r + BLOCK, :]
                for t in range(2):
                    f = t * levels + l
                    base = TOP + r
                    q = s[f, base : base + BLOCK, :]
                    far = jnp.where(ee <= 0.0, pltpu.roll(q, 1, 1), pltpu.roll(q, cols - 2, 1))
                    flux = ea * q + eb * pltpu.roll(q, cols - 1, 1) + ee * far
                    total = q - flux + pltpu.roll(flux, 1, 1)
                    a = s[f, base - 1 : base + BLOCK - 1, :]
                    c = s[f, base + 1 : base + BLOCK + 1, :]
                    d = s[f, base + 2 : base + BLOCK + 2, :]
                    flux = na * q + nb * c + ne * jnp.where(ne <= 0.0, a, d)
                    flow[t, 8 + r : 8 + r + BLOCK, :] = flux
                    total = total - flux + flow[t, 7 + r : 7 + r + BLOCK, :]
                    put(t, l, r, o * total)
            return carry

        lax.fori_loop(0, levels, level, 0)

    def put_s1(t, l, r, value):
        s1[t * levels + l, TOP + r : TOP + r + BLOCK, :] = value

    def put_out(t, l, r, value):
        out[t, l, r : r + BLOCK, :] = value

    def rows_fixed(step, s, add):
        @pl.when(northern)
        def _():
            picked = rf[step][lax.div(fold_ref[0], jnp.int32(cols))]
            north_rows[...] = reversed_lanes(picked)

        @pl.when(jnp.logical_not(northern))
        def _():
            north_rows[...] = rn[step, 0:12]

        o0, o1 = ocean[:, 0:1, :], ocean[:, 1:2, :]
        oy, oz = ocean[:, rows - 2 : rows - 1, :], ocean[:, rows - 1 : rows, :]
        above = jnp.where(northern, oz, rn[0, 12:15])
        below = jnp.where(southern, 0.0, rs[0, 18:21])
        first = o0 * o1 * jnp.maximum(nc[:, 0:1, :], 0.0) * (-1.0 / 6.0)
        last = oy * oz * jnp.minimum(nc[:, rows - 2 : rows - 1, :], 0.0) * (-1.0 / 6.0)
        for t in range(2):
            part = slice(t * levels, (t + 1) * levels)
            part2 = slice((2 + t) * levels, (3 + t) * levels)
            q0, q1 = s[part, TOP : TOP + 1, :], s[part, TOP + 1 : TOP + 2, :]
            qy = s[part, TOP + rows - 2 : TOP + rows - 1, :]
            qz = s[part, TOP + rows - 1 : TOP + rows, :]
            m2 = jnp.where(southern, 0.0, rs[step, part])
            m1 = jnp.where(southern, 0.0, rs[step, part2])
            p0, p1 = north_rows[part], north_rows[part2]
            low = face_flux(
                m2, m1, q0, q1, jnp.where(southern, 0.0, rs[0, 12:15]),
                jnp.where(southern, 0.0, rs[0, 15:18]), below * o0,
            )
            high = face_flux(
                qy, qz, p0, p1, nc[:, rows - 1 : rows, :], nk[:, rows - 1 : rows, :], oz * above
            )
            enters = first * m1
            leaves = last * p0
            add(t, 0, o0 * (low - enters))
            add(t, 1, o1 * enters)
            add(t, rows - 2, -oy * leaves)
            add(t, rows - 1, oz * (leaves - high))

    def columns_fixed(step, tq):
        for h in halves:
            oy, oz, o0, o1 = [column(t0, h, j, n, levels) for j in range(4)]
            cy, cz, c0, _ = [column(t0, h, j, n + levels, levels) for j in range(4)]
            kz = column(t0, h, 1, n + 2 * levels, levels)
            om = rw[0, h, 2 * n : 2 * n + levels]
            cm = rw[0, h, 2 * n + levels : 2 * n + 2 * levels]
            km = rw[0, h, 2 * n + 2 * levels : 2 * n + 3 * levels]
            op = re[0, h, 2 * n : 2 * n + levels]
            first = o0 * o1 * jnp.maximum(c0, 0.0) * (-1.0 / 6.0)
            last = oy * oz * jnp.minimum(cy, 0.0) * (-1.0 / 6.0)
            for t in range(2):
                qy, qz, q0, q1 = [column(tq, h, j, t * levels, levels) for j in range(4)]
                m2 = rw[step, h, t * levels : (t + 1) * levels]
                m1 = rw[step, h, n + t * levels : n + (t + 1) * levels]
                p0 = re[step, h, t * levels : (t + 1) * levels]
                p1 = re[step, h, n + t * levels : n + (t + 1) * levels]
                low = face_flux(m2, m1, q0, q1, cm, km, om * o0)
                high = face_flux(qy, qz, p0, p1, cz, kz, oz * op)
                enters = first * m1
                leaves = last * p0
                for j, fix in enumerate(
                    (-oy * leaves, oz * (leaves - high), o0 * (low - enters), o1 * enters)
                ):
                    ct[h, pl.ds(4 * t * levels + j, levels, stride=4), :] = fix

    def turn_columns():
        for h in halves:
            ce[h * cols : (h + 1) * cols, :] = ct[h].T

    def spread_columns(add, blocks):
        edge = (lane < 2) | (lane >= cols - 2)
        for f in range(n):
            for r in blocks:
                x = ce[r : r + BLOCK, :]
                add(f, r, jnp.where(edge, pltpu.roll(x, (cols - 4 * f - 2) % cols, 1), 0.0))

    advance(s0, put_s1)
    for h in halves:
        ct[h] = jnp.zeros((cols, cols), F32)
    wait_lat(0)
    to_east(0).wait()
    to_west(0).wait()

    def add_row_s1(t, r, value):
        part = slice(t * levels, (t + 1) * levels)
        s1[part, TOP + r : TOP + r + 1, :] = s1[part, TOP + r : TOP + r + 1, :] + value

    rows_fixed(0, s0, add_row_s1)
    columns_fixed(0, t0)
    pack([(s1, f, TOP) for f in range(n)], t1)
    for h in halves:
        t1[h, 0 : 4 * n] = t1[h, 0 : 4 * n] + ct[h, 0 : 4 * n]
        se[1, h, 0:n] = column(t1, h, 0, 0, n)
        se[1, h, n : 2 * n] = column(t1, h, 1, 0, n)
        sw[1, h, 0:n] = column(t1, h, 2, 0, n)
        sw[1, h, n : 2 * n] = column(t1, h, 3, 0, n)
    to_east(1).start()
    to_west(1).start()

    def add_s1(f, r, value):
        at = slice(TOP + r, TOP + r + BLOCK)
        s1[f, at, :] = s1[f, at, :] + value

    turn_columns()
    spread_columns(add_s1, (starts[0], starts[-1]))
    fill_rows(1, s1)
    start_lat(1)
    spread_columns(add_s1, starts[1:-1])
    advance(s1, put_out)
    wait_lat(1)
    to_east(1).wait()
    to_west(1).wait()

    def add_row_out(t, r, value):
        out[t, :, r : r + 1, :] = out[t, :, r : r + 1, :] + value

    rows_fixed(1, s1, add_row_out)
    columns_fixed(1, t1)

    def add_out(f, r, value):
        t, l = divmod(f, levels)
        out[t, l, r : r + BLOCK, :] = out[t, l, r : r + BLOCK, :] + value

    turn_columns()
    spread_columns(add_out, starts)


def local(tracers, east_courant, north_courant, east_kappa, north_kappa, ocean_mask, fold_map):
    nlat = lax.axis_size("lat")
    nlon = lax.axis_size("lon")
    levels, rows, cols = ocean_mask.shape
    fields = 2 * levels
    halves = rows // cols

    def scratch(*shape):
        return pltpu.VMEM(shape, F32)

    return pl.pallas_call(
        functools.partial(kernel, nlat, nlon),
        out_shape=pltpu.VMEM(tracers.shape, F32),
        in_specs=[pl.BlockSpec(memory_space=pltpu.SMEM)] + [pl.BlockSpec(memory_space=pltpu.HBM)] * 6,
        out_specs=pl.BlockSpec(memory_space=pltpu.VMEM),
        scratch_shapes=[
            scratch(2, levels, rows, cols),
            scratch(levels, rows, cols),
            scratch(levels, rows, cols),
            scratch(levels, rows, cols),
            scratch(levels, rows, cols),
            pltpu.VMEM((levels, rows, cols), jnp.int32),
            scratch(2, rows + 8, cols),
            pltpu.SemaphoreType.DMA((6,)),
            scratch(fields, TOP + rows + 8, cols),
            scratch(fields, TOP + rows + 8, cols),
            scratch(levels, rows + 8, cols),
            scratch(3, levels, rows, cols),
            scratch(3, levels, rows, cols),
            scratch(rows, cols),
            scratch(halves, cols, cols),
            scratch(halves, cols, cols),
            scratch(halves, cols, cols),
            scratch(rows, cols),
            scratch(2, halves, 24, cols),
            scratch(2, halves, 16, cols),
            scratch(2, 21, 1, cols),
            scratch(2, 15, 1, cols),
            scratch(2, 12, 1, cols),
            scratch(2, halves, 16, cols),
            scratch(2, halves, 24, cols),
            scratch(2, 15, 1, cols),
            scratch(2, 21, 1, cols),
            scratch(nlon, 12, 1, cols),
            scratch(nlon, 12, 1, cols),
            scratch(12, 1, cols),
            pltpu.SemaphoreType.DMA((2, 4)),
            pltpu.SemaphoreType.DMA((2, 4)),
            pltpu.SemaphoreType.DMA((2, nlon - 1)),
            pltpu.SemaphoreType.DMA((2, nlon - 1)),
        ],
        compiler_params=pltpu.CompilerParams(
            collective_id=0, has_side_effects=True, vmem_limit_bytes=55 * 1024 * 1024
        ),
    )(
        fold_map,
        *(
            pltpu.with_memory_space_constraint(x, pltpu.HBM)
            for x in (tracers, east_courant, north_courant, east_kappa, north_kappa, ocean_mask)
        ),
    )


def solution(mesh):
    in_specs = (
        P(None, None, "lat", "lon"),
        P(None, "lat", "lon"),
        P(None, "lat", "lon"),
        P(None, "lat", "lon"),
        P(None, "lat", "lon"),
        P(None, "lat", "lon"),
        P("lon"),
    )
    out_specs = P(None, None, "lat", "lon")
    return jax.shard_map(local, mesh=mesh, in_specs=in_specs, out_specs=out_specs, check_vma=False)
```
